32 devices in a mesh: groups: 2 (over x), tlo: 8 (over z, y), thi: 2 (over core).
Axes of the slice: x: 2, y: 2, z: 4, core: 2. Of those that a mesh axis runs over, the one named last changes fastest.
Arguments:
- diagonal_blocks: float32 [32, 512, 512], P(('groups', 'tlo', 'thi')), parts along dimension 0, may hold values from -1 to 8, as said below
- coupling_blocks: float32 [32, 512, 512], P(('groups', 'tlo', 'thi')), parts along dimension 0, may hold values from -3.5 to 0.5
- arrow_blocks: float32 [32, 512, 128], P(('groups', 'tlo', 'thi')), parts along dimension 0, may hold values from -1 to 1
- block_rhs: float32 [32, 512, 256], P(('groups', 'tlo', 'thi')), parts along dimension 0, may hold values from -6 to 6
- tip_block: float32 [256, 128], P('groups'), parts along dimension 0, may hold values from -2 to 26, as said below
- tip_rhs: float32 [256, 256], P('groups'), parts along dimension 0, may hold values from -6 to 6
Outputs:
- chol_factor: float32 [32, 512, 512], P(('groups', 'tlo', 'thi')), parts along dimension 0
- left_factor: float32 [32, 512, 512], P(('groups', 'tlo', 'thi')), parts along dimension 0
- right_factor: float32 [32, 512, 512], P(('groups', 'tlo', 'thi')), parts along dimension 0
- arrow_factor: float32 [32, 512, 128], P(('groups', 'tlo', 'thi')), parts along dimension 0
- forward_rhs: float32 [32, 512, 256], P(('groups', 'tlo', 'thi')), parts along dimension 0
- tip_factor: float32 [256, 128], P('groups'), parts along dimension 0
- tip_solved: float32 [256, 256], P('groups'), parts along dimension 0
- logdet_mean: float32 [2], P('groups'), parts along dimension 0
The draws below stay inside these ranges and needn't reach their ends.
There are 2 independent parts, one for each index of `groups`. The reference program is written for one: setup_inputs(seed, part) draws one part's arguments, and reference() takes and returns one part's arrays. A program takes and returns all parts, laid end to end along the dimension named above; each array names one. Nothing has to cross between parts.
Inputs may be any that keep to these rules, and one draw needn't show every extreme that they name: `diagonal_blocks`: each diagonal block is symmetric; with coupling_blocks, arrow_blocks and tip_block the blocks form a symmetric positive definite matrix. tip_block is symmetric.
All inputs are finite; a program needn't handle non-finite values.
Results may differ from the reference program's by a relative error of at most 0.0003.
Values sent between devices are 32-bit elements; how exact they have to be, the bound alone decides.
A program may use at most 192 MiB of HBM per device.

```python
import math
import jax
import jax.numpy as jnp
import numpy as np
from jax import lax

BLOCK = 512
FIXED = 128
PROBES = 256
BLOCKS = 16


def symmetric_noise(key, count, order, spread):
    raw = jax.random.uniform(key, (count, order, order), jnp.float32, -1.0, 1.0)
    return (raw + jnp.swapaxes(raw, 1, 2)) * (spread * 0.70710678)


def interface_law(key):
    first, second, third, fourth = jax.random.split(jax.random.fold_in(key, 21), 4)
    spatial_diag = jax.random.uniform(first, (BLOCKS, BLOCK), jnp.float32, 1.6, 3.2)
    noise = symmetric_noise(second, BLOCKS, BLOCK, 0.866 / math.sqrt(BLOCK))
    identity = jnp.eye(BLOCK, dtype=jnp.float32)
    spatial = noise + identity[None, :, :] * spatial_diag[:, :, None]
    rho = jax.random.uniform(third, (BLOCKS,), jnp.float32, 0.95, 0.995)
    nugget_draw = jax.random.uniform(fourth, (BLOCKS, BLOCK), jnp.float32)
    nugget = 0.005 * jnp.exp(math.log(200.0) * nugget_draw)
    return (spatial, rho, nugget)


def draw_diagonal_blocks(key, part):
    spatial, rho, nugget = interface_law(key)
    previous = jnp.roll(spatial, 1, axis=0)
    identity = jnp.eye(BLOCK, dtype=jnp.float32)
    return (rho * rho)[:, None, None] * spatial + previous + identity[None, :, :] * nugget[:, :, None]


def draw_coupling_blocks(key, part):
    spatial, rho, nugget = interface_law(key)
    return -rho[:, None, None] * spatial


def draw_arrow_blocks(key, part):
    first, second, third = jax.random.split(jax.random.fold_in(key, 13), 3)
    shuffled = jax.random.permutation(third, FIXED)
    home_block = shuffled % BLOCKS
    owner = (home_block[None, :] == jnp.arange(BLOCKS)[:, None]).astype(jnp.float32)
    shape_all = (BLOCKS, BLOCK, FIXED)
    base_part = jax.random.truncated_normal(first, -4.0, 4.0, shape_all, jnp.float32)
    spike_part = jax.random.truncated_normal(second, -4.0, 4.0, shape_all, jnp.float32)
    base_scale = 0.7 / math.sqrt(BLOCKS * BLOCK)
    spike_scale = 1.0 / math.sqrt(BLOCK)
    return base_part * base_scale + spike_part * spike_scale * owner[:, None, :]


def draw_tip_block(key, part):
    first, second = jax.random.split(jax.random.fold_in(key, 14))
    diagonal_law = jax.random.uniform(first, (FIXED,), jnp.float32, 1.0, 1.5)
    noise = symmetric_noise(second, 1, FIXED, 4.33 / math.sqrt(FIXED))[0]
    identity = jnp.eye(FIXED, dtype=jnp.float32)
    return noise + identity * (16.0 * diagonal_law)[:, None]


def block_scale(rng, shape, shards, least, high):
    def one(position, shards_of):
        steps = jax.random.uniform(jax.random.fold_in(jax.random.fold_in(rng, 6), position), (shards_of,), jnp.float32, least / len(shards), high / len(shards))
        return jnp.repeat(jnp.exp(steps), shape[position] // shards_of).reshape((-1,) + (1,) * (len(shape) - position - 1))

    level = one(*shards[0])
    for cut in shards[1:]:
        level = level * one(*cut)
    return level


def bell_draw(key, extent, width, most, shards=(), kind=jnp.bfloat16):
    result = jax.random.normal(key, extent, jnp.float32) * width
    if len(shards) > 0:
        result = block_scale(key, extent, shards, -0.22, 0.18) * result
    return jnp.clip(result, min=-most, max=most).astype(kind)


def setup_inputs(seed: int = 0, part: int = 0) -> dict:
    key_list = jax.random.split(jax.random.key(seed), 7)
    part_splits = jax.random.split(jax.random.fold_in(key_list[6], part), 7)
    return {
        "diagonal_blocks": draw_diagonal_blocks(jax.random.fold_in(jax.random.fold_in(key_list[6], part), 71), part),
        "coupling_blocks": draw_coupling_blocks(jax.random.fold_in(jax.random.fold_in(key_list[6], part), 71), part),
        "arrow_blocks": draw_arrow_blocks(jax.random.fold_in(jax.random.fold_in(key_list[6], part), 71), part),
        "block_rhs": bell_draw(part_splits[3], (BLOCKS, BLOCK, PROBES), 1.0, 6.0, ((0, 16),), jnp.float32),
        "tip_block": draw_tip_block(jax.random.fold_in(jax.random.fold_in(key_list[6], part), 71), part),
        "tip_rhs": bell_draw(part_splits[5], (FIXED, PROBES), 1.0, 6.0, (), jnp.float32),
    }


def lower_solve(factor, right_side):
    return lax.linalg.triangular_solve(factor, right_side, left_side=True, lower=True)

def batch_outer(first_part, whole_part):
    return jnp.einsum('jbr,jbc->jrc', first_part, whole_part, precision=lax.Precision.HIGHEST)

def reference(diagonal_blocks, coupling_blocks, arrow_blocks, block_rhs, tip_block, tip_rhs):
    total_blocks = BLOCKS
    levels = total_blocks.bit_length() - 1
    half_blocks = total_blocks // 2
    block_width = BLOCK
    tip_width = FIXED
    pivots = diagonal_blocks
    couplings = coupling_blocks.at[total_blocks - 1].set(jnp.zeros_like(coupling_blocks[0]))
    arrows = arrow_blocks
    targets = block_rhs
    chol_out = jnp.zeros_like(pivots)
    left_out = jnp.zeros_like(pivots)
    right_out = jnp.zeros_like(pivots)
    arrow_out = jnp.zeros_like(arrows)
    target_out = jnp.zeros_like(targets)
    tip_terms = jnp.zeros((tip_width, tip_width + PROBES), jnp.float32)
    log_total = jnp.zeros((), jnp.float32)
    positions = np.arange(total_blocks)
    ordinals = positions + half_blocks
    for level_index in range(levels + 1):
        stride = 1 << level_index
        if level_index < levels:
            chosen = positions[(ordinals % stride == 0) & (ordinals // stride % 2 == 1)]
        else:
            chosen = np.array([half_blocks])
        left_ids = chosen - stride
        has_left = left_ids >= 0
        left_blocks = jnp.where(jnp.asarray(has_left)[:, None, None], jnp.swapaxes(couplings[np.maximum(left_ids, 0)], 1, 2), 0.0)
        panel_all = jnp.concatenate([left_blocks, couplings[chosen], arrows[chosen], targets[chosen]], axis=2)
        factors = jnp.linalg.cholesky(pivots[chosen])
        solved = lower_solve(factors, panel_all)
        chol_out = chol_out.at[chosen].set(factors)
        left_out = left_out.at[chosen].set(solved[:, :, :block_width])
        right_out = right_out.at[chosen].set(solved[:, :, block_width:2 * block_width])
        arrow_out = arrow_out.at[chosen].set(solved[:, :, 2 * block_width:2 * block_width + tip_width])
        target_out = target_out.at[chosen].set(solved[:, :, 2 * block_width + tip_width:])
        tail_part = solved[:, :, 2 * block_width:]
        tip_terms = tip_terms + jnp.einsum('jba,jbc->ac', tail_part[:, :, :tip_width], tail_part, precision=lax.Precision.HIGHEST)
        log_total = log_total + 2.0 * jnp.sum(jnp.log(jnp.diagonal(factors, axis1=1, axis2=2)))
        if level_index < levels:
            keep = np.arange(chosen.shape[0])[has_left]
            if keep.shape[0] > 0:
                from_left = solved[keep]
                update = batch_outer(from_left[:, :, :block_width], from_left)
                target_ids = left_ids[keep]
                pivots = pivots.at[target_ids].add(-update[:, :, :block_width])
                couplings = couplings.at[target_ids].set(-update[:, :, block_width:2 * block_width])
                arrows = arrows.at[target_ids].add(-update[:, :, 2 * block_width:2 * block_width + tip_width])
                targets = targets.at[target_ids].add(-update[:, :, 2 * block_width + tip_width:])
            right_ids = chosen + stride
            keep_right = np.arange(chosen.shape[0])[right_ids <= total_blocks - 1]
            if keep_right.shape[0] > 0:
                from_right = solved[keep_right]
                update = batch_outer(from_right[:, :, block_width:2 * block_width], from_right[:, :, block_width:])
                target_ids = right_ids[keep_right]
                pivots = pivots.at[target_ids].add(-update[:, :, :block_width])
                arrows = arrows.at[target_ids].add(-update[:, :, block_width:block_width + tip_width])
                targets = targets.at[target_ids].add(-update[:, :, block_width + tip_width:])
    reduced = tip_block - tip_terms[:, :tip_width]
    tip_target = tip_rhs - tip_terms[:, tip_width:]
    tip_factor = jnp.linalg.cholesky(reduced)
    tip_solved = lower_solve(tip_factor, tip_target)
    logdet_mean = (log_total + 2.0 * jnp.sum(jnp.log(jnp.diagonal(tip_factor)))) / (total_blocks * block_width + tip_width)
    return (chol_out, left_out, right_out, arrow_out, target_out, tip_factor, tip_solved, logdet_mean.reshape(1))
```

```python
import functools

import jax
import jax.numpy as jnp
from jax import lax
from jax.experimental import pallas as pl
from jax.experimental.pallas import tpu as pltpu
from jax.sharding import PartitionSpec as P

TILE = 128
ROWS = 8
PANEL = 4
PRECISE = lax.Precision.HIGHEST


def dot_nn(a, b):
    return lax.dot_general(
        a, b, (((1,), (0,)), ((), ())), precision=PRECISE, preferred_element_type=jnp.float32
    )


def dot_nt(a, b):
    return lax.dot_general(
        a, b, (((1,), (1,)), ((), ())), precision=PRECISE, preferred_element_type=jnp.float32
    )


def dot_tn(a, b):
    return lax.dot_general(
        a, b, (((0,), (0,)), ((), ())), precision=PRECISE, preferred_element_type=jnp.float32
    )


def tile_factor(tile):
    chunks = TILE // ROWS
    row_id = lax.broadcasted_iota(jnp.int32, (TILE, TILE), 0)
    col_id = lax.broadcasted_iota(jnp.int32, (TILE, TILE), 1)
    eye = (row_id == col_id).astype(jnp.float32)
    sub_id = lax.broadcasted_iota(jnp.int32, (ROWS, TILE), 0)
    work = [tile[ROWS * c : ROWS * (c + 1)] for c in range(chunks)]
    back = [eye[ROWS * c : ROWS * (c + 1)] for c in range(chunks)]

    def whole(row):
        return jnp.broadcast_to(row, (ROWS, TILE))

    for first in range(0, TILE, PANEL):
        home, sub = first // ROWS, first % ROWS
        cols = [
            {c: whole(work[c][:, first + k : first + k + 1]) for c in range(home, chunks)}
            for k in range(PANEL)
        ]
        rows = [whole(work[home][sub + k : sub + k + 1]) for k in range(PANEL)]
        backs = [whole(back[home][sub + k : sub + k + 1]) for k in range(PANEL)]
        piv = [[whole(cols[b][home][sub + a : sub + a + 1]) for b in range(PANEL)] for a in range(PANEL)]
        inv = []
        for k in range(PANEL):
            inv.append(1.0 / piv[k][k])
            for a in range(k + 1, PANEL):
                f = piv[a][k] * inv[k]
                rows[a] = rows[a] - f * rows[k]
                backs[a] = backs[a] - f * backs[k]
                for b in range(k + 1, PANEL):
                    piv[a][b] = piv[a][b] - f * piv[k][b]
        for c in range(home, chunks):
            for k in range(PANEL):
                f = cols[k][c] * inv[k]
                if c == home:
                    f = jnp.where(sub_id > sub + k, f, 0.0)
                work[c] = work[c] - f * rows[k]
                back[c] = back[c] - f * backs[k]
                for b in range(k + 1, PANEL):
                    cols[b][c] = cols[b][c] - f * piv[k][b]
    reduced = jnp.concatenate(work, axis=0)
    pivots = jnp.sum(jnp.where(row_id == col_id, reduced, 0.0), axis=1, keepdims=True)
    scale = 1.0 / jnp.sqrt(pivots)
    upper = jnp.where(col_id >= row_id, reduced * scale, 0.0)
    return upper, jnp.concatenate(back, axis=0) * scale


def factor_kernel(s_ref, l_ref, v_ref, a_ref):
    order = s_ref.shape[0]
    a_ref[...] = s_ref[...]

    @pl.loop(0, order // TILE)
    def _(step):
        here = pl.ds(pl.multiple_of(step * TILE, TILE), TILE)
        upper, inverse = tile_factor(a_ref[here, here])
        v_ref[here, :] = inverse
        if order > TILE:
            below = lax.broadcasted_iota(jnp.int32, (order, TILE), 0) >= (step + 1) * TILE
            column = jnp.where(below, dot_nt(a_ref[:, here], inverse), 0.0)
            l_ref[:, here] = column
            a_ref[...] = a_ref[...] - dot_nt(column, column)
        l_ref[here, here] = upper.T


def factor(pivot):
    order = pivot.shape[0]
    return pl.pallas_call(
        factor_kernel,
        out_shape=(
            jax.ShapeDtypeStruct((order, order), jnp.float32),
            jax.ShapeDtypeStruct((order, TILE), jnp.float32),
        ),
        in_specs=[pl.BlockSpec(memory_space=pltpu.VMEM)],
        out_specs=(pl.BlockSpec(memory_space=pltpu.VMEM),) * 2,
        scratch_shapes=[pltpu.VMEM((order, order), jnp.float32)],
        compiler_params=pltpu.CompilerParams(vmem_limit_bytes=32 * 1024 * 1024),
        cost_estimate=pl.CostEstimate(flops=20000000000, bytes_accessed=2 * 4 * order * order, transcendentals=0),
        name="factor",
    )(pivot)


def solve_kernel(count, l_ref, v_ref, *refs):
    order = l_ref.shape[0]
    for src, dst in zip(refs[:count], refs[count:]):
        for k in range(order // TILE):
            at = slice(k * TILE, (k + 1) * TILE)
            part = src[at, :]
            if k > 0:
                part = part - dot_nn(l_ref[at, : k * TILE], dst[: k * TILE, :])
            dst[at, :] = dot_nn(v_ref[at, :], part)


def solve(low, inverse, sides):


    count = len(sides)
    return pl.pallas_call(
        functools.partial(solve_kernel, count),
        out_shape=tuple(jax.ShapeDtypeStruct(s.shape, jnp.float32) for s in sides),
        in_specs=[pl.BlockSpec(memory_space=pltpu.VMEM)] * (2 + count),
        out_specs=(pl.BlockSpec(memory_space=pltpu.VMEM),) * count,
        compiler_params=pltpu.CompilerParams(vmem_limit_bytes=32 * 1024 * 1024),
        cost_estimate=pl.CostEstimate(flops=5000000000, bytes_accessed=8000000, transcendentals=0),
        name="solve",
    )(low, inverse, *sides)


def shifted(array, by):
    size = lax.axis_size(("tlo", "thi"))
    pairs = [(i, i + by) for i in range(size) if 0 <= i + by < size]
    return lax.ppermute(array, ("tlo", "thi"), pairs)


def log_diagonal(matrix):
    row_id = lax.broadcasted_iota(jnp.int32, matrix.shape, 0)
    col_id = lax.broadcasted_iota(jnp.int32, matrix.shape, 1)
    return 2.0 * jnp.sum(jnp.log(jnp.sum(jnp.where(row_id == col_id, matrix, 0.0), axis=1)))


def body(diagonal_blocks, coupling_blocks, arrow_blocks, block_rhs, tip_block, tip_rhs):
    pivot = diagonal_blocks[0]
    arrow = arrow_blocks[0]
    target = block_rhs[0]
    width = pivot.shape[0]
    tip_width = arrow.shape[1]
    partitions = lax.axis_size(("tlo", "thi"))
    levels = partitions.bit_length() - 1
    half = partitions // 2
    position = lax.axis_index(("tlo", "thi"))
    ordinal = position + half
    last = partitions - 1
    upper = jnp.where(position == last, 0.0, coupling_blocks[0])
    lower = jnp.where(position >= 1, shifted(upper, 1).T, 0.0)
    kept = None
    for level in range(levels + 1):
        stride = 1 << level
        final = level == levels
        if final:
            chosen = position == half
        else:
            chosen = (ordinal % stride == 0) & (ordinal // stride % 2 == 1)
        between = (ordinal % stride == 0) & (ordinal // stride % 2 == 0)
        takes_left = between & (position + stride <= last)
        takes_right = between & (position >= stride)
        with_left = level + 2 <= levels
        low, inverse = factor(pivot)
        sides = [arrow, target]
        if not final:
            sides.append(upper)
        if with_left:
            sides.append(lower)
        solved = list(solve(low, inverse, sides))
        m_arrow, m_target = solved[:2]
        zero = jnp.zeros((width, width), jnp.float32)
        m_right = zero if final else solved[2]
        m_left = solved[3] if with_left else zero
        now = (low, m_left, m_right, m_arrow, m_target)
        kept = now if kept is None else tuple(jnp.where(chosen, n, k) for n, k in zip(now, kept))
        if final:
            break
        if with_left:
            from_left = shifted(dot_tn(m_left, m_left), -stride)
        from_right = shifted(dot_tn(m_right, m_right), stride)
        if with_left:
            pivot = pivot - jnp.where(takes_left, from_left, 0.0)
        pivot = pivot - jnp.where(takes_right, from_right, 0.0)
        tail = jnp.concatenate([m_arrow, m_target], axis=1)
        if with_left:
            new_upper = shifted(dot_tn(m_left, m_right), -stride)
            new_lower = shifted(dot_tn(m_right, m_left), stride)
            left_tail = shifted(dot_tn(m_left, tail), -stride)
            arrow = arrow - jnp.where(takes_left, left_tail[:, :tip_width], 0.0)
            target = target - jnp.where(takes_left, left_tail[:, tip_width:], 0.0)
            upper = jnp.where(takes_left, -new_upper, upper)
            lower = jnp.where(takes_right, -new_lower, 0.0)
        right_tail = shifted(dot_tn(m_right, tail), stride)
        arrow = arrow - jnp.where(takes_right, right_tail[:, :tip_width], 0.0)
        target = target - jnp.where(takes_right, right_tail[:, tip_width:], 0.0)
    chol_part, left_part, right_part, arrow_part, target_part = kept
    terms = dot_tn(arrow_part, jnp.concatenate([arrow_part, target_part], axis=1))
    totals, log_total = lax.psum((terms, log_diagonal(chol_part)), ("tlo", "thi"))
    tip_factor, tip_inverse = factor(tip_block - totals[:, :tip_width])
    tip_solved = dot_nn(tip_inverse, tip_rhs - totals[:, tip_width:])
    unknowns = partitions * width + tip_width
    logdet_mean = (log_total + log_diagonal(tip_factor)) / unknowns
    return (
        chol_part[None],
        left_part[None],
        right_part[None],
        arrow_part[None],
        target_part[None],
        tip_factor,
        tip_solved,
        logdet_mean.reshape(1),
    )


def solution(mesh):
    blocks = P(("groups", "tlo", "thi"), None, None)
    tips = P("groups", None)
    return jax.shard_map(
        body,
        mesh=mesh,
        in_specs=(blocks,) * 4 + (tips,) * 2,
        out_specs=(blocks,) * 5 + (tips, tips, P("groups")),
        check_vma=False,
    )
```

```python
import functools

import jax
import jax.numpy as jnp
from jax import lax
from jax.experimental import pallas as pl
from jax.experimental.pallas import tpu as pltpu
from jax.sharding import PartitionSpec as P

TILE = 128
ROWS = 8
PANEL = 4
PRECISE = lax.Precision.HIGHEST


def dot_nn(a, b):
    return lax.dot_general(
        a, b, (((1,), (0,)), ((), ())), precision=PRECISE, preferred_element_type=jnp.float32
    )


def dot_nt(a, b):
    return lax.dot_general(
        a, b, (((1,), (1,)), ((), ())), precision=PRECISE, preferred_element_type=jnp.float32
    )


def dot_tn(a, b):
    return lax.dot_general(
        a, b, (((0,), (0,)), ((), ())), precision=PRECISE, preferred_element_type=jnp.float32
    )


def tile_factor(tile):
    chunks = TILE // ROWS
    row_id = lax.broadcasted_iota(jnp.int32, (TILE, TILE), 0)
    col_id = lax.broadcasted_iota(jnp.int32, (TILE, TILE), 1)
    eye = (row_id == col_id).astype(jnp.float32)
    sub_id = lax.broadcasted_iota(jnp.int32, (ROWS, TILE), 0)
    work = [tile[ROWS * c : ROWS * (c + 1)] for c in range(chunks)]
    back = [eye[ROWS * c : ROWS * (c + 1)] for c in range(chunks)]

    def whole(row):
        return jnp.broadcast_to(row, (ROWS, TILE))

    for first in range(0, TILE, PANEL):
        home, sub = first // ROWS, first % ROWS
        cols = [
            {c: whole(work[c][:, first + k : first + k + 1]) for c in range(home, chunks)}
            for k in range(PANEL)
        ]
        rows = [whole(work[home][sub + k : sub + k + 1]) for k in range(PANEL)]
        backs = [whole(back[home][sub + k : sub + k + 1]) for k in range(PANEL)]
        piv = [[whole(cols[b][home][sub + a : sub + a + 1]) for b in range(PANEL)] for a in range(PANEL)]
        inv = []
        for k in range(PANEL):
            inv.append(1.0 / piv[k][k])
            for a in range(k + 1, PANEL):
                f = piv[a][k] * inv[k]
                rows[a] = rows[a] - f * rows[k]
                backs[a] = backs[a] - f * backs[k]
                for b in range(k + 1, PANEL):
                    piv[a][b] = piv[a][b] - f * piv[k][b]
        for c in range(home, chunks):
            for k in range(PANEL):
                f = cols[k][c] * inv[k]
                if c == home:
                    f = jnp.where(sub_id > sub + k, f, 0.0)
                work[c] = work[c] - f * rows[k]
                back[c] = back[c] - f * backs[k]
                for b in range(k + 1, PANEL):
                    cols[b][c] = cols[b][c] - f * piv[k][b]
    reduced = jnp.concatenate(work, axis=0)
    pivots = jnp.sum(jnp.where(row_id == col_id, reduced, 0.0), axis=1, keepdims=True)
    scale = 1.0 / jnp.sqrt(pivots)
    upper = jnp.where(col_id >= row_id, reduced * scale, 0.0)
    return upper, jnp.concatenate(back, axis=0) * scale


def factor_kernel(s_ref, l_ref, v_ref, a_ref):
    order = s_ref.shape[0]
    a_ref[...] = s_ref[...]

    @pl.loop(0, order // TILE)
    def _(step):
        here = pl.ds(pl.multiple_of(step * TILE, TILE), TILE)
        upper, inverse = tile_factor(a_ref[here, here])
        v_ref[here, :] = inverse
        if order > TILE:
            below = lax.broadcasted_iota(jnp.int32, (order, TILE), 0) >= (step + 1) * TILE
            column = jnp.where(below, dot_nt(a_ref[:, here], inverse), 0.0)
            l_ref[:, here] = column
            a_ref[...] = a_ref[...] - dot_nt(column, column)
        l_ref[here, here] = upper.T


def factor(pivot):
    order = pivot.shape[0]
    return pl.pallas_call(
        factor_kernel,
        out_shape=(
            jax.ShapeDtypeStruct((order, order), jnp.float32),
            jax.ShapeDtypeStruct((order, TILE), jnp.float32),
        ),
        in_specs=[pl.BlockSpec(memory_space=pltpu.VMEM)],
        out_specs=(pl.BlockSpec(memory_space=pltpu.VMEM),) * 2,
        scratch_shapes=[pltpu.VMEM((order, order), jnp.float32)],
        compiler_params=pltpu.CompilerParams(vmem_limit_bytes=32 * 1024 * 1024),
        cost_estimate=pl.CostEstimate(flops=35000000000, bytes_accessed=2 * 4 * order * order, transcendentals=0),
        name="factor",
    )(pivot)


def solve_kernel(count, l_ref, v_ref, *refs):
    order = l_ref.shape[0]
    for src, dst in zip(refs[:count], refs[count:]):
        for k in range(order // TILE):
            at = slice(k * TILE, (k + 1) * TILE)
            part = src[at, :]
            if k > 0:
                part = part - dot_nn(l_ref[at, : k * TILE], dst[: k * TILE, :])
            dst[at, :] = dot_nn(v_ref[at, :], part)


def solve(low, inverse, sides):


    count = len(sides)
    return pl.pallas_call(
        functools.partial(solve_kernel, count),
        out_shape=tuple(jax.ShapeDtypeStruct(s.shape, jnp.float32) for s in sides),
        in_specs=[pl.BlockSpec(memory_space=pltpu.VMEM)] * (2 + count),
        out_specs=(pl.BlockSpec(memory_space=pltpu.VMEM),) * count,
        compiler_params=pltpu.CompilerParams(vmem_limit_bytes=32 * 1024 * 1024),
        cost_estimate=pl.CostEstimate(flops=5000000000, bytes_accessed=8000000, transcendentals=0),
        name="solve",
    )(low, inverse, *sides)


def shifted(array, by, senders):
    size = lax.axis_size(("tlo", "thi"))
    pairs = [(i, i + by) for i in senders if 0 <= i + by < size]
    return lax.ppermute(array, ("tlo", "thi"), pairs)


def spread(array, root):
    holders = [root]
    bit = lax.axis_size(("tlo", "thi")) // 2
    while bit > 0:
        others = [i ^ bit for i in holders]
        array = array + lax.ppermute(array, ("tlo", "thi"), list(zip(holders, others)))
        holders = holders + others
        bit //= 2
    return array


def tip_message(chol_part, arrow_part, target_part, here):
    terms = dot_tn(arrow_part, jnp.concatenate([arrow_part, target_part], axis=1))
    logs = jnp.broadcast_to(log_diagonal(chol_part), (ROWS, terms.shape[1]))
    return jnp.where(here, jnp.concatenate([terms, logs], axis=0), 0.0)


def log_diagonal(matrix):
    row_id = lax.broadcasted_iota(jnp.int32, matrix.shape, 0)
    col_id = lax.broadcasted_iota(jnp.int32, matrix.shape, 1)
    return 2.0 * jnp.sum(jnp.log(jnp.sum(jnp.where(row_id == col_id, matrix, 0.0), axis=1)))


def body(diagonal_blocks, coupling_blocks, arrow_blocks, block_rhs, tip_block, tip_rhs):
    pivot = diagonal_blocks[0]
    arrow = arrow_blocks[0]
    target = block_rhs[0]
    width = pivot.shape[0]
    tip_width = arrow.shape[1]
    partitions = lax.axis_size(("tlo", "thi"))
    levels = partitions.bit_length() - 1
    half = partitions // 2
    position = lax.axis_index(("tlo", "thi"))
    ordinal = position + half
    last = partitions - 1
    upper = jnp.where(position == last, 0.0, coupling_blocks[0])
    first_level = [i for i in range(partitions) if (i + half) % 2 == 1]
    lower = shifted(upper, 1, [i - 1 for i in first_level if i >= 1]).T
    kept = None
    for level in range(levels + 1):
        stride = 1 << level
        final = level == levels
        senders = [i for i in range(partitions) if (i + half) % (2 * stride) == stride]
        if final:
            chosen = position == half
        else:
            chosen = (ordinal % stride == 0) & (ordinal // stride % 2 == 1)
        between = (ordinal % stride == 0) & (ordinal // stride % 2 == 0)
        takes_left = between & (position + stride <= last)
        with_left = level + 2 <= levels
        low, inverse = factor(pivot)
        sides = [arrow, target]
        if not final:
            sides.append(upper)
        if with_left:
            sides.append(lower)
        solved = list(solve(low, inverse, sides))
        m_arrow, m_target = solved[:2]
        zero = jnp.zeros((width, width), jnp.float32)
        m_right = zero if final else solved[2]
        m_left = solved[3] if with_left else zero
        now = (low, m_left, m_right, m_arrow, m_target)
        kept = now if kept is None else tuple(jnp.where(chosen, n, k) for n, k in zip(now, kept))
        if final:
            break
        if level == levels - 1:
            early = tip_message(kept[0], kept[3], kept[4], position != half)
            early = lax.psum(early, ("tlo", "thi"))
        if with_left:
            from_left = shifted(dot_tn(m_left, m_left), -stride, senders)
        from_right = shifted(dot_tn(m_right, m_right), stride, senders)
        if with_left:
            pivot = pivot - from_left
        pivot = pivot - from_right
        tail = jnp.concatenate([m_arrow, m_target], axis=1)
        if with_left:
            new_upper = shifted(dot_tn(m_left, m_right), -stride, senders)
            new_lower = shifted(dot_tn(m_right, m_left), stride, senders)
            left_tail = shifted(dot_tn(m_left, tail), -stride, senders)
            arrow = arrow - left_tail[:, :tip_width]
            target = target - left_tail[:, tip_width:]
            upper = jnp.where(takes_left, -new_upper, upper)
            lower = -new_lower
        right_tail = shifted(dot_tn(m_right, tail), stride, senders)
        arrow = arrow - right_tail[:, :tip_width]
        target = target - right_tail[:, tip_width:]
    chol_part, left_part, right_part, arrow_part, target_part = kept
    late = tip_message(low, m_arrow, m_target, position == half)
    totals = early + spread(late, half)
    log_total = totals[tip_width, 0]
    totals = totals[:tip_width]
    tip_factor, tip_inverse = factor(tip_block - totals[:, :tip_width])
    tip_solved = dot_nn(tip_inverse, tip_rhs - totals[:, tip_width:])
    unknowns = partitions * width + tip_width
    logdet_mean = (log_total + log_diagonal(tip_factor)) / unknowns
    return (
        chol_part[None],
        left_part[None],
        right_part[None],
        arrow_part[None],
        target_part[None],
        tip_factor,
        tip_solved,
        logdet_mean.reshape(1),
    )


def solution(mesh):
    blocks = P(("groups", "tlo", "thi"), None, None)
    tips = P("groups", None)
    return jax.shard_map(
        body,
        mesh=mesh,
        in_specs=(blocks,) * 4 + (tips,) * 2,
        out_specs=(blocks,) * 5 + (tips, tips, P("groups")),
        check_vma=False,
    )
```

```python
import functools

import jax
import jax.numpy as jnp
from jax import lax
from jax.experimental import pallas as pl
from jax.experimental.pallas import tpu as pltpu
from jax.sharding import PartitionSpec as P

TILE = 128
ROWS = 8
PANEL = 4
PRECISE = lax.Precision.HIGHEST


def dot_nn(a, b):
    return lax.dot_general(
        a, b, (((1,), (0,)), ((), ())), precision=PRECISE, preferred_element_type=jnp.float32
    )


def dot_nt(a, b):
    return lax.dot_general(
        a, b, (((1,), (1,)), ((), ())), precision=PRECISE, preferred_element_type=jnp.float32
    )


def dot_tn(a, b):
    return lax.dot_general(
        a, b, (((0,), (0,)), ((), ())), precision=PRECISE, preferred_element_type=jnp.float32
    )


def tile_factor(tile):
    chunks = TILE // ROWS
    row_id = lax.broadcasted_iota(jnp.int32, (TILE, TILE), 0)
    col_id = lax.broadcasted_iota(jnp.int32, (TILE, TILE), 1)
    eye = (row_id == col_id).astype(jnp.float32)
    sub_id = lax.broadcasted_iota(jnp.int32, (ROWS, TILE), 0)
    work = [tile[ROWS * c : ROWS * (c + 1)] for c in range(chunks)]
    back = [eye[ROWS * c : ROWS * (c + 1)] for c in range(chunks)]

    def whole(row):
        return jnp.broadcast_to(row, (ROWS, TILE))

    for first in range(0, TILE, PANEL):
        home, sub = first // ROWS, first % ROWS
        cols = [
            {c: whole(work[c][:, first + k : first + k + 1]) for c in range(home, chunks)}
            for k in range(PANEL)
        ]
        rows = [whole(work[home][sub + k : sub + k + 1]) for k in range(PANEL)]
        backs = [whole(back[home][sub + k : sub + k + 1]) for k in range(PANEL)]
        piv = [[whole(cols[b][home][sub + a : sub + a + 1]) for b in range(PANEL)] for a in range(PANEL)]
        inv = []
        for k in range(PANEL):
            inv.append(1.0 / piv[k][k])
            for a in range(k + 1, PANEL):
                f = piv[a][k] * inv[k]
                rows[a] = rows[a] - f * rows[k]
                backs[a] = backs[a] - f * backs[k]
                for b in range(k + 1, PANEL):
                    piv[a][b] = piv[a][b] - f * piv[k][b]
        for c in range(home, chunks):
            for k in range(PANEL):
                f = cols[k][c] * inv[k]
                if c == home:
                    f = jnp.where(sub_id > sub + k, f, 0.0)
                work[c] = work[c] - f * rows[k]
                back[c] = back[c] - f * backs[k]
                for b in range(k + 1, PANEL):
                    cols[b][c] = cols[b][c] - f * piv[k][b]
    reduced = jnp.concatenate(work, axis=0)
    pivots = jnp.sum(jnp.where(row_id == col_id, reduced, 0.0), axis=1, keepdims=True)
    scale = 1.0 / jnp.sqrt(pivots)
    upper = jnp.where(col_id >= row_id, reduced * scale, 0.0)
    return upper, jnp.concatenate(back, axis=0) * scale


def factor_kernel(s_ref, l_ref, v_ref, a_ref):
    order = s_ref.shape[0]
    a_ref[...] = s_ref[...]

    @pl.loop(0, order // TILE)
    def _(step):
        here = pl.ds(pl.multiple_of(step * TILE, TILE), TILE)
        upper, inverse = tile_factor(a_ref[here, here])
        v_ref[here, :] = inverse
        if order > TILE:
            below = lax.broadcasted_iota(jnp.int32, (order, TILE), 0) >= (step + 1) * TILE
            column = jnp.where(below, dot_nt(a_ref[:, here], inverse), 0.0)
            l_ref[:, here] = column
            a_ref[...] = a_ref[...] - dot_nt(column, column)
        l_ref[here, here] = upper.T


def factor(pivot):
    order = pivot.shape[0]
    return pl.pallas_call(
        factor_kernel,
        out_shape=(
            jax.ShapeDtypeStruct((order, order), jnp.float32),
            jax.ShapeDtypeStruct((order, TILE), jnp.float32),
        ),
        in_specs=[pl.BlockSpec(memory_space=pltpu.VMEM)],
        out_specs=(pl.BlockSpec(memory_space=pltpu.VMEM),) * 2,
        scratch_shapes=[pltpu.VMEM((order, order), jnp.float32)],
        compiler_params=pltpu.CompilerParams(vmem_limit_bytes=32 * 1024 * 1024),
        cost_estimate=pl.CostEstimate(flops=35000000000, bytes_accessed=2 * 4 * order * order, transcendentals=0),
        name="factor",
    )(pivot)


def solve_kernel(count, l_ref, v_ref, *refs):
    order = l_ref.shape[0]
    for src, dst in zip(refs[:count], refs[count:]):
        for k in range(order // TILE):
            at = slice(k * TILE, (k + 1) * TILE)
            part = src[at, :]
            if k > 0:
                part = part - dot_nn(l_ref[at, : k * TILE], dst[: k * TILE, :])
            dst[at, :] = dot_nn(v_ref[at, :], part)


def solve(low, inverse, sides):


    count = len(sides)
    return pl.pallas_call(
        functools.partial(solve_kernel, count),
        out_shape=tuple(jax.ShapeDtypeStruct(s.shape, jnp.float32) for s in sides),
        in_specs=[pl.BlockSpec(memory_space=pltpu.VMEM)] * (2 + count),
        out_specs=(pl.BlockSpec(memory_space=pltpu.VMEM),) * count,
        compiler_params=pltpu.CompilerParams(vmem_limit_bytes=32 * 1024 * 1024),
        cost_estimate=pl.CostEstimate(flops=5000000000, bytes_accessed=8000000, transcendentals=0),
        name="solve",
    )(low, inverse, *sides)


def shifted(array, by, senders):
    size = lax.axis_size(("tlo", "thi"))
    pairs = [(i, i + by) for i in senders if 0 <= i + by < size]
    return lax.ppermute(array, ("tlo", "thi"), pairs)


def spread(array, root):
    holders = [root]
    bit = lax.axis_size(("tlo", "thi")) // 2
    while bit > 0:
        others = [i ^ bit for i in holders]
        array = array + lax.ppermute(array, ("tlo", "thi"), list(zip(holders, others)))
        holders = holders + others
        bit //= 2
    return array


def tip_message(chol_part, arrow_part, target_part):
    terms = dot_tn(arrow_part, jnp.concatenate([arrow_part, target_part], axis=1))
    logs = jnp.broadcast_to(log_diagonal(chol_part), (ROWS, terms.shape[1]))
    return jnp.concatenate([terms, logs], axis=0)


def log_diagonal(matrix):
    row_id = lax.broadcasted_iota(jnp.int32, matrix.shape, 0)
    col_id = lax.broadcasted_iota(jnp.int32, matrix.shape, 1)
    return 2.0 * jnp.sum(jnp.log(jnp.sum(jnp.where(row_id == col_id, matrix, 0.0), axis=1)))


def body(diagonal_blocks, coupling_blocks, arrow_blocks, block_rhs, tip_block, tip_rhs):
    pivot = diagonal_blocks[0]
    arrow = arrow_blocks[0]
    target = block_rhs[0]
    width = pivot.shape[0]
    tip_width = arrow.shape[1]
    partitions = lax.axis_size(("tlo", "thi"))
    levels = partitions.bit_length() - 1
    half = partitions // 2
    position = lax.axis_index(("tlo", "thi"))
    ordinal = position + half
    last = partitions - 1
    upper = jnp.where(position == last, 0.0, coupling_blocks[0])
    first_level = [i for i in range(partitions) if (i + half) % 2 == 1]
    lower = shifted(upper, 1, [i - 1 for i in first_level if i >= 1]).T
    kept = None
    gathered = jnp.zeros((tip_width + ROWS, tip_width + target.shape[1]), jnp.float32)
    for level in range(levels + 1):
        stride = 1 << level
        final = level == levels
        senders = [i for i in range(partitions) if (i + half) % (2 * stride) == stride]
        if final:
            chosen = position == half
        else:
            chosen = (ordinal % stride == 0) & (ordinal // stride % 2 == 1)
        between = (ordinal % stride == 0) & (ordinal // stride % 2 == 0)
        takes_left = between & (position + stride <= last)
        with_left = level + 2 <= levels
        low, inverse = factor(pivot)
        sides = [arrow, target]
        if not final:
            sides.append(upper)
        if with_left:
            sides.append(lower)
        solved = list(solve(low, inverse, sides))
        m_arrow, m_target = solved[:2]
        zero = jnp.zeros((width, width), jnp.float32)
        m_right = zero if final else solved[2]
        m_left = solved[3] if with_left else zero
        now = (low, m_left, m_right, m_arrow, m_target)
        kept = now if kept is None else tuple(jnp.where(chosen, n, k) for n, k in zip(now, kept))
        if final:
            break
        if with_left:
            from_left = shifted(dot_tn(m_left, m_left), -stride, senders)
        from_right = shifted(dot_tn(m_right, m_right), stride, senders)
        if with_left:
            pivot = pivot - from_left
        pivot = pivot - from_right
        tail = jnp.concatenate([m_arrow, m_target], axis=1)
        message = gathered + tip_message(low, m_arrow, m_target)
        if with_left:
            pivot, to_upper, to_lower, to_left, to_right, message = lax.optimization_barrier(
                (
                    pivot,
                    dot_tn(m_left, m_right),
                    dot_tn(m_right, m_left),
                    dot_tn(m_left, tail),
                    dot_tn(m_right, tail),
                    message,
                )
            )
            upper = jnp.where(takes_left, -shifted(to_upper, -stride, senders), upper)
            lower = -shifted(to_lower, stride, senders)
            left_tail = shifted(to_left, -stride, senders)
            arrow = arrow - left_tail[:, :tip_width]
            target = target - left_tail[:, tip_width:]
        else:
            pivot, to_right, message = lax.optimization_barrier(
                (pivot, dot_tn(m_right, tail), message)
            )
        right_tail = shifted(to_right, stride, senders)
        arrow = arrow - right_tail[:, :tip_width]
        target = target - right_tail[:, tip_width:]
        gathered = gathered + shifted(message, -stride if with_left else stride, senders)
    chol_part, left_part, right_part, arrow_part, target_part = kept
    totals = gathered + tip_message(low, m_arrow, m_target)
    totals = spread(jnp.where(position == half, totals, 0.0), half)
    log_total = totals[tip_width, 0]
    totals = totals[:tip_width]
    tip_factor, tip_inverse = factor(tip_block - totals[:, :tip_width])
    tip_solved = dot_nn(tip_inverse, tip_rhs - totals[:, tip_width:])
    unknowns = partitions * width + tip_width
    logdet_mean = (log_total + log_diagonal(tip_factor)) / unknowns
    return (
        chol_part[None],
        left_part[None],
        right_part[None],
        arrow_part[None],
        target_part[None],
        tip_factor,
        tip_solved,
        logdet_mean.reshape(1),
    )


def solution(mesh):
    blocks = P(("groups", "tlo", "thi"), None, None)
    tips = P("groups", None)
    return jax.shard_map(
        body,
        mesh=mesh,
        in_specs=(blocks,) * 4 + (tips,) * 2,
        out_specs=(blocks,) * 5 + (tips, tips, P("groups")),
        check_vma=False,
    )
```
